256 devices in a mesh: grp: 32 (over z, x_hi, core), blk: 8 (over y, x_lo).
Axes of the slice: x: 4 (x_hi: 2, x_lo: 2; x = x_hi * 2 + x_lo), y: 4, z: 8, core: 2. Of those that a mesh axis runs over, the one named last changes fastest.
Arguments:
- tiles: float32 [1024, 512, 512], P(('grp', 'blk')), as said below
- pairs: int32 [1024, 2], P(('grp', 'blk')), may hold values from 0 to 255, as said below
- direction: float32 [32, 32, 8, 512], P(None, None, 'blk'), may hold values from -6 to 6
Outputs:
- image: float32 [32, 32, 8, 512], P(None, 'grp', 'blk')
The draws below stay inside these ranges and needn't reach their ends.
Inputs may be any that keep to these rules, and one draw needn't show every extreme that they name: Rows d * 4 to (d + 1) * 4 - 1 of pairs hold pairs (i, j) with i // 8 == d // 8 and j % 8 == d % 8; no unordered pair appears twice; a pair with i < j has i + j even, one with i > j has i + j odd. `tiles`: A tile whose pair has i == j is symmetric.
All inputs are finite; a program needn't handle non-finite values.
Results may differ from the reference program's by a relative error of at most 0.0003.
Values sent between devices are 32-bit elements; how exact they have to be, the bound alone decides.
No kernel may reach another device: no remote copies, remote signals or barrier semaphores. Data moves between devices by JAX's collectives and lax.ppermute only.
A program may use at most 64 MiB of HBM per device.

```python
import jax
import jax.numpy as jnp
from jax import lax

COLS = 32
TB = 512
K = 4
NB = 256
N_GRP = 32
N_BLK = 8


def pair_table(key):
    count = N_GRP * N_BLK
    cand = jnp.arange(count, dtype=jnp.int32)
    rows_r = cand // N_GRP
    cols_m = cand % N_GRP

    def for_device(device):
        group_at = device // N_BLK
        block_at = device % N_BLK
        row_block = group_at * N_BLK + rows_r
        col_block = cols_m * N_BLK + block_at
        parity = (row_block + col_block) % 2
        upper = (row_block < col_block) & (parity == 0)
        lower = (row_block > col_block) & (parity == 1)
        usable = (upper | lower | (row_block == col_block)).astype(jnp.int32)
        scores = jax.random.permutation(jax.random.fold_in(key, device), count).astype(jnp.int32)
        scores = scores + count * (1 - usable)
        order = jnp.argsort(scores, stable=True)[:K]
        return jnp.stack([row_block[order], col_block[order]], axis=1)
    table = jax.vmap(for_device)(jnp.arange(count, dtype=jnp.int32))
    return table.reshape(count * K, 2).astype(jnp.int32)


def draw_pairs(key, part):
    return pair_table(jax.random.fold_in(key, 11))


def draw_tiles(key, part):
    table = pair_table(jax.random.fold_in(key, 11))
    shape = (N_GRP * N_BLK * K, TB, TB)
    base = jax.random.normal(jax.random.fold_in(key, 5), shape, jnp.float32)
    scale = (2.0 * K * TB) ** (-0.5)
    symmetric = (base + jnp.swapaxes(base, 1, 2)) * 0.7071
    on_diag = (table[:, 0] == table[:, 1])[:, None, None]
    return (jnp.where(on_diag, symmetric, base) * scale).astype(jnp.float32)


def block_scale(rng, shape, split, least, high):
    level, own = 1.0, jax.random.fold_in(rng, 6)
    for axis_at, shards_of in split:
        draws = jnp.exp(jax.random.uniform(jax.random.fold_in(own, axis_at), (shards_of,), jnp.float32, least / len(split), high / len(split)))
        level = level * jnp.repeat(draws, shape[axis_at] // shards_of).reshape([-1 if axis == axis_at else 1 for axis in range(len(shape))])
    return level


def noise(own_key, extent, scale, most, cuts=(), kind=jnp.bfloat16):
    result = jax.random.normal(own_key, extent, jnp.float32) * scale
    if len(cuts) > 0:
        result = block_scale(own_key, extent, cuts, -0.22, 0.18) * result
    return jnp.clip(result, min=-most, max=most).astype(kind)


def setup_inputs(seed: int = 0) -> dict:
    key_of = jax.random.split(jax.random.key(seed), 4)
    return {
        "tiles": draw_tiles(jax.random.fold_in(key_of[3], 71), 0),
        "pairs": draw_pairs(jax.random.fold_in(key_of[3], 71), 0),
        "direction": noise(key_of[2], (COLS, N_GRP, N_BLK, TB), 1.0, 6.0, ((2, 8),), jnp.float32),
    }


def reference(tiles, pairs, direction):
    flat = direction.reshape(COLS, NB, TB)
    groups = tiles.reshape(N_GRP * N_BLK, K, TB, TB)
    group_pairs = pairs.reshape(N_GRP * N_BLK, K, 2)

    def add_group(total, item):
        blocks, index = item
        rows_at = index[:, 0].astype(jnp.int32)
        cols_at = index[:, 1].astype(jnp.int32)
        right = flat[:, cols_at]
        left = flat[:, rows_at]
        row_terms = jnp.einsum("ckt,kst->cks", right, blocks, precision=lax.Precision.HIGHEST)
        mirror = jnp.einsum("cks,kst->ckt", left, blocks, precision=lax.Precision.HIGHEST)
        keep = (rows_at != cols_at).astype(flat.dtype)
        mirror = mirror * keep[None, :, None]
        total = total.at[:, rows_at].add(row_terms)
        total = total.at[:, cols_at].add(mirror)
        return total, None

    start = jnp.zeros((COLS, NB, TB), dtype=flat.dtype)
    total, unused = lax.scan(add_group, start, (groups, group_pairs))
    return total.reshape(COLS, N_GRP, N_BLK, TB)
```

```python
import jax
import jax.numpy as jnp
from jax import lax
from jax.experimental import pallas as pl
from jax.experimental.pallas import tpu as pltpu
from jax.sharding import PartitionSpec as P

BLKS = 8
GRPS = 32
ZS = 8
VMEM_BYTES = 40 * 1024 * 1024
VMEM_WHOLE = 62 * 1024 * 1024


def split(x):
    high = x.astype(jnp.bfloat16)
    low = (x - high.astype(jnp.float32)).astype(jnp.bfloat16)
    return high, low


def product(p, tile, contract):
    count = p.shape[0]
    p_parts = jnp.concatenate(split(p), axis=0)
    t_high, t_low = split(tile)
    dims = (((1,), (contract,)), ((), ()))
    first = lax.dot_general(p_parts, t_high, dims, preferred_element_type=jnp.float32)
    second = lax.dot_general(p_parts, t_low, dims, preferred_element_type=jnp.float32)
    both = first + second
    return both[:count] + both[count:]


def rows_kernel(pairs, direction, tiles, out, held, own, picked, tile_sem, pick_sem):
    k_count = tiles.shape[0]
    cols = own.shape[0]
    grp = pairs[0, 0] // BLKS
    own_copy = pltpu.make_async_copy(direction.at[:, grp], own, pick_sem.at[k_count])
    own_copy.start()
    picks, loads = [], []
    for k in range(k_count):
        picks.append(
            pltpu.make_async_copy(direction.at[:, pairs[1, k] // BLKS], picked.at[k], pick_sem.at[k])
        )
        picks[k].start()
        loads.append(pltpu.make_async_copy(tiles.at[k], held.at[k], tile_sem.at[k]))
        loads[k].start()
    own_copy.wait()
    mine = jnp.concatenate([own[:, q, :] for q in range(4)], axis=1)
    for r in range(BLKS):
        out[r, :cols] = mine
        out[r, cols:] = jnp.zeros_like(mine)
    for k in range(k_count):
        picks[k].wait()
        loads[k].wait()
        p = jnp.concatenate([picked[k, :, q, :] for q in range(4)], axis=1)
        r = pairs[0, k] % BLKS
        out[r, cols:] += product(p, held[k], 1)


def mirror_kernel(pairs, got, tiles, send, stay, row_sum):
    k_count = tiles.shape[0]
    cols = row_sum.shape[0]
    x_mine = (pairs[0, 0] // BLKS) // 2 % 2
    total = got[0, cols:]
    for b in range(1, BLKS):
        total = total + got[b, cols:]
    row_sum[...] = total
    for k in range(k_count):
        i, j = pairs[0, k], pairs[1, k]
        m = j // BLKS
        value = product(got[i % BLKS, :cols], tiles[k], 0)
        value = jnp.where(i != j, value, 0.0)
        stay[k] = value
        send[pl.ds(k * cols, cols)] = value
        place = jnp.where(m // 2 % 2 != x_mine, m // 4 * 2 + m % 2, -1).astype(jnp.float32)
        send[k_count * cols:, pl.ds(k * 128, 128)] = jnp.full((8, 128), place, jnp.float32)


def place_kernel(pairs, stay, came, send, keep):
    k_count, cols, width = stay.shape
    grp = pairs[0, 0] // BLKS
    core = grp % 2
    x_mine = grp // 2 % 2
    send[...] = jnp.zeros_like(send)
    keep[...] = jnp.zeros_like(keep)

    def add(place, value):
        z = place // 2

        @pl.when((place >= 0) & (place % 2 == core))
        def _():
            keep[z] += value

        @pl.when((place >= 0) & (place % 2 != core))
        def _():
            send[z] += value

    for k in range(k_count):
        m = pairs[1, k] // BLKS
        add(jnp.where(m // 2 % 2 == x_mine, m // 4 * 2 + m % 2, -1), stay[k])
        place = jnp.max(came[k_count * cols:, pl.ds(k * 128, 128)]).astype(jnp.int32)
        add(place, came[pl.ds(k * cols, cols)])


def shards(tiles, pairs, direction):
    k_count, width, _ = tiles.shape
    cols = direction.shape[0]
    f32 = jnp.float32
    smem = pl.BlockSpec(memory_space=pltpu.SMEM)
    vmem = pl.BlockSpec(memory_space=pltpu.VMEM)
    hbm = pl.BlockSpec(memory_space=pltpu.HBM)
    params = pltpu.CompilerParams(vmem_limit_bytes=VMEM_BYTES)
    pairs = pairs.T
    lanes = direction.reshape(cols, GRPS, 4, 128)
    first = pl.pallas_call(
        rows_kernel,
        out_shape=jax.ShapeDtypeStruct((BLKS, 2 * cols, width), f32),
        in_specs=[smem, hbm, hbm],
        out_specs=vmem,
        scratch_shapes=[
            pltpu.VMEM((k_count, width, width), f32),
            pltpu.VMEM((cols, 4, 128), f32),
            pltpu.VMEM((k_count, cols, 4, 128), f32),
            pltpu.SemaphoreType.DMA((k_count,)),
            pltpu.SemaphoreType.DMA((k_count + 1,)),
        ],
        compiler_params=pltpu.CompilerParams(vmem_limit_bytes=VMEM_WHOLE),
        name="rows",
    )(pairs, lanes, tiles)
    got = lax.all_to_all(first, "blk", 0, 0, tiled=True)
    send, stay, row_sum = pl.pallas_call(
        mirror_kernel,
        out_shape=[
            jax.ShapeDtypeStruct((k_count * cols + 8, width), f32),
            jax.ShapeDtypeStruct((k_count, cols, width), f32),
            jax.ShapeDtypeStruct((cols, width), f32),
        ],
        in_specs=[smem, vmem, vmem],
        out_specs=[vmem, vmem, vmem],
        compiler_params=params,
        name="mirror",
    )(pairs, got, tiles)
    came = lax.ppermute(send, "grp", [(g, g ^ 2) for g in range(GRPS)])
    send, keep = pl.pallas_call(
        place_kernel,
        out_shape=[jax.ShapeDtypeStruct((ZS, cols, width), f32)] * 2,
        in_specs=[smem, vmem, vmem],
        out_specs=[vmem, vmem],
        compiler_params=params,
        name="place",
    )(pairs, stay, came)
    came = lax.ppermute(send, "grp", [(g, g ^ 1) for g in range(GRPS)])
    part = keep + came
    along_z = [[z * 4 + q for z in range(ZS)] for q in range(4)]
    parts = lax.all_to_all(part, "grp", 0, 0, tiled=True, axis_index_groups=along_z)
    return (jnp.sum(parts, axis=0) + row_sum).reshape(cols, 1, 1, width)


def solution(mesh):
    placed = (P(("grp", "blk"), None, None), P(("grp", "blk"), None), P(None, None, "blk", None))
    return jax.shard_map(
        shards, mesh=mesh, in_specs=placed, out_specs=P(None, "grp", "blk", None), check_vma=False
    )
```

```python
import jax
import jax.numpy as jnp
from jax import lax
from jax.experimental import pallas as pl
from jax.experimental.pallas import tpu as pltpu
from jax.sharding import PartitionSpec as P

BLKS = 8
GRPS = 32
ZS = 8
YS = 4
VMEM_BYTES = 32 * 1024 * 1024


def split(x):
    high = x.astype(jnp.bfloat16)
    low = (x - high.astype(jnp.float32)).astype(jnp.bfloat16)
    return high, low


def product(p, tile, contract):
    count = p.shape[0]
    p_parts = jnp.concatenate(split(p), axis=0)
    t_high, t_low = split(tile)
    dims = (((1,), (contract,)), ((), ()))
    first = lax.dot_general(p_parts, t_high, dims, preferred_element_type=jnp.float32)
    second = lax.dot_general(p_parts, t_low, dims, preferred_element_type=jnp.float32)
    both = first + second
    return both[:count] + both[count:]


def joined(ref):
    return jnp.concatenate([ref[:, q, :] for q in range(4)], axis=1)


def own_kernel(direction, out, own, sem):
    copy = pltpu.make_async_copy(direction.at[:, lax.axis_index("grp")], own, sem)
    copy.start()
    copy.wait()
    mine = joined(own)
    for r in range(BLKS):
        out[r] = mine


def rows_kernel(pairs, direction, tiles, out, kept, rest, picked, tile_sem, pick_sem):
    k_count = tiles.shape[0]
    held = [kept.at[k] for k in range(kept.shape[0])] + [rest.at[k] for k in range(rest.shape[0])]
    picks, loads = [], []
    for k in range(k_count):
        picks.append(
            pltpu.make_async_copy(direction.at[:, pairs[1, k] // BLKS], picked.at[k], pick_sem.at[k])
        )
        picks[k].start()
        loads.append(pltpu.make_async_copy(tiles.at[k], held[k], tile_sem.at[k]))
        loads[k].start()
    out[...] = jnp.zeros_like(out)
    for k in range(k_count):
        picks[k].wait()
        loads[k].wait()
        r, b = pairs[0, k] % BLKS, pairs[1, k] % BLKS
        out[(r + b) % 2, (r // 2 + YS - b // 2) % YS] += product(joined(picked.at[k]), held[k][...], 1)


def mirror_kernel(pairs, got, kept, tiles, out, rest, tile_sem):
    k_count = tiles.shape[0]
    cols = got.shape[1]
    near = kept.shape[0]
    loads = []
    for k in range(near, k_count):
        loads.append(pltpu.make_async_copy(tiles.at[k], rest.at[k - near], tile_sem.at[k - near]))
        loads[-1].start()
    for k in range(k_count):
        if k >= near:
            loads[k - near].wait()
        tile = kept[k] if k < near else rest[k - near]
        i, j = pairs[0, k], pairs[1, k]
        out[pl.ds(k * cols, cols)] = product(got[i % BLKS], tile, 0)
        place = jnp.where(i != j, j // BLKS, -1).astype(jnp.float32)
        out[k_count * cols:, pl.ds(k * 128, 128)] = jnp.full((8, 128), place, jnp.float32)


def place_kernel(pairs, *refs):
    *parts, out = refs
    cols, width = out.shape[1:]
    k_count = width // 128
    mine = pairs[0, 0] // BLKS % 4
    groups = [jnp.where(pairs[0, k] != pairs[1, k], pairs[1, k] // BLKS, -1) for k in range(k_count)]
    for part in parts[1:]:
        for k in range(k_count):
            groups.append(part[pl.ds(k_count * cols, 1), pl.ds(k * 128, 128)][0, 0].astype(jnp.int32))
    out[...] = jnp.zeros_like(out)
    for at, part in enumerate(parts):
        for k in range(k_count):
            m = groups[at * k_count + k]

            @pl.when((m >= 0) & (m % 4 == mine))
            def _():
                out[m // 4] += part[pl.ds(k * cols, cols)]


def shards(tiles, pairs, direction):
    k_count, width, _ = tiles.shape
    cols = direction.shape[0]
    f32 = jnp.float32
    smem = pl.BlockSpec(memory_space=pltpu.SMEM)
    vmem = pl.BlockSpec(memory_space=pltpu.VMEM)
    hbm = pl.BlockSpec(memory_space=pltpu.HBM)
    params = pltpu.CompilerParams(vmem_limit_bytes=VMEM_BYTES)
    pairs = pairs.T
    lanes = pltpu.with_memory_space_constraint(direction.reshape(cols, GRPS, 4, 128), pltpu.HBM)
    own = pl.pallas_call(
        own_kernel,
        out_shape=jax.ShapeDtypeStruct((BLKS, cols, width), f32),
        in_specs=[hbm],
        out_specs=vmem,
        scratch_shapes=[pltpu.VMEM((cols, 4, 128), f32), pltpu.SemaphoreType.DMA],
        compiler_params=params,
        name="own",
    )(lanes)
    got = lax.all_to_all(own, "blk", 0, 0, tiled=True)
    near = k_count // 2
    tiles = pltpu.with_memory_space_constraint(tiles, pltpu.HBM)
    rows, kept = pl.pallas_call(
        rows_kernel,
        out_shape=[
            jax.ShapeDtypeStruct((2, YS, cols, width), f32),
            jax.ShapeDtypeStruct((near, width, width), f32),
        ],
        in_specs=[smem, hbm, hbm],
        out_specs=[vmem, vmem],
        scratch_shapes=[
            pltpu.VMEM((k_count - near, width, width), f32),
            pltpu.VMEM((k_count, cols, 4, 128), f32),
            pltpu.SemaphoreType.DMA((k_count,)),
            pltpu.SemaphoreType.DMA((k_count,)),
        ],
        compiler_params=params,
        cost_estimate=pl.CostEstimate(flops=600_000_000, bytes_accessed=10_000_000, transcendentals=0),
        name="rows",
    )(pairs, lanes, tiles)
    rows = rows[0] + lax.ppermute(rows[1], "blk", [(b, b ^ 1) for b in range(BLKS)])
    terms = pl.pallas_call(
        mirror_kernel,
        out_shape=jax.ShapeDtypeStruct((k_count * cols + 8, width), f32),
        in_specs=[smem, vmem, vmem, hbm],
        out_specs=vmem,
        scratch_shapes=[
            pltpu.VMEM((k_count - near, width, width), f32),
            pltpu.SemaphoreType.DMA((k_count - near,)),
        ],
        compiler_params=params,
        name="mirror",
    )(pairs, got, kept, tiles)
    over_x = lax.ppermute(terms, "grp", [(g, g ^ 2) for g in range(GRPS)])
    over_core = lax.ppermute(terms, "grp", [(g, g ^ 1) for g in range(GRPS)])
    over_both = lax.ppermute(over_x, "grp", [(g, g ^ 1) for g in range(GRPS)])
    part = pl.pallas_call(
        place_kernel,
        out_shape=jax.ShapeDtypeStruct((ZS, cols, width), f32),
        in_specs=[smem, vmem, vmem, vmem, vmem],
        out_specs=vmem,
        compiler_params=params,
        name="place",
    )(pairs, terms, over_core, over_x, over_both)
    along_z = [[z * 4 + q for z in range(ZS)] for q in range(4)]
    parts = lax.all_to_all(part, "grp", 0, 0, tiled=True, axis_index_groups=along_z)
    total = rows[0]
    for step in range(1, YS):
        total = total + lax.ppermute(rows[step], "blk", [(b, (b + 2 * step) % BLKS) for b in range(BLKS)])
    total = total + jnp.sum(parts, axis=0)
    return total.reshape(cols, 1, 1, width)


def solution(mesh):
    placed = (P(("grp", "blk"), None, None), P(("grp", "blk"), None), P(None, None, "blk", None))
    return jax.shard_map(
        shards, mesh=mesh, in_specs=placed, out_specs=P(None, "grp", "blk", None), check_vma=False
    )
```

```python
import jax
import jax.numpy as jnp
from jax import lax
from jax.experimental import pallas as pl
from jax.experimental.pallas import tpu as pltpu
from jax.sharding import PartitionSpec as P

BLKS = 8
GRPS = 32
ZS = 8
YS = 4
Z_ORDER = (4, 3, 5, 2, 6, 1, 7)
Z_AFTER = {1: 2, 7: 6}
VMEM_BYTES = 32 * 1024 * 1024


def split(x):
    high = x.astype(jnp.bfloat16)
    low = (x - high.astype(jnp.float32)).astype(jnp.bfloat16)
    return high, low


def product(p, tile, contract):
    count = p.shape[0]
    p_parts = jnp.concatenate(split(p), axis=0)
    t_high, t_low = split(tile)
    dims = (((1,), (contract,)), ((), ()))
    first = lax.dot_general(p_parts, t_high, dims, preferred_element_type=jnp.float32)
    second = lax.dot_general(p_parts, t_low, dims, preferred_element_type=jnp.float32)
    both = first + second
    return both[:count] + both[count:]


def joined(ref):
    return jnp.concatenate([ref[:, q, :] for q in range(4)], axis=1)


def own_kernel(direction, out, own, sem):
    copy = pltpu.make_async_copy(direction.at[:, lax.axis_index("grp")], own, sem)
    copy.start()
    copy.wait()
    out[...] = joined(own)


def rows_kernel(pairs, direction, tiles, out, held, picked, sem):
    k_count = tiles.shape[0]
    picks, loads = [], []
    for k in range(k_count):
        group = pairs[1, k] // BLKS
        picks.append(pltpu.make_async_copy(direction.at[:, group], picked.at[k], sem.at[0, k]))
        loads.append(pltpu.make_async_copy(tiles.at[k], held.at[k], sem.at[1, k]))
        picks[k].start()
        loads[k].start()
    out[...] = jnp.zeros_like(out)
    for k in range(k_count):
        picks[k].wait()
        loads[k].wait()
        out[pairs[0, k] % BLKS] += product(joined(picked.at[k]), held[k], 1)


def mirror_kernel(pairs, *refs):
    *got, tiles, out, held = refs
    k_count = tiles.shape[0]
    cols = got[0].shape[0]
    b = pairs[1, 0] % BLKS
    for k in range(k_count):
        i, j = pairs[0, k], pairs[1, k]
        r = i % BLKS
        source = (b // 2 + YS - r // 2) % YS * 2 + (r + b) % 2
        for at, block in enumerate(got):

            @pl.when(source == at)
            def _():
                held[k] = block[...]

        out[pl.ds(k * cols, cols)] = product(held[k], tiles[k], 0)
        place = jnp.where(i != j, j // BLKS, -1).astype(jnp.float32)
        out[k_count * cols:, pl.ds(k * 128, 128)] = jnp.full((8, 128), place, jnp.float32)


def group_of(part, k, k_count, cols):
    return part[pl.ds(k_count * cols, 1), pl.ds(k * 128, 128)][0, 0].astype(jnp.int32)


def add_parts(grp, groups, parts, out):
    cols = out.shape[1]
    k_count = len(groups) // len(parts)
    for at, m in enumerate(groups):

        @pl.when((m >= 0) & (m % 4 == grp % 4))
        def _():
            out[(m // 4 + ZS - grp // 4) % ZS] += parts[at // k_count][pl.ds(at % k_count * cols, cols)]


def place_kernel(pairs, own, other, out):
    cols, width = out.shape[1:]
    k_count = width // 128
    groups = [jnp.where(pairs[0, k] != pairs[1, k], pairs[1, k] // BLKS, -1) for k in range(k_count)]
    groups += [group_of(other, k, k_count, cols) for k in range(k_count)]
    out[...] = jnp.zeros_like(out)
    add_parts(pairs[0, 0] // BLKS, groups, [own, other], out)


def join_kernel(pairs, base, one, two, *refs):
    *outs, total = refs
    cols, width = total.shape[1:]
    k_count = width // 128
    groups = [group_of(part, k, k_count, cols) for part in (one, two) for k in range(k_count)]
    total[...] = base[...]
    add_parts(pairs[0, 0] // BLKS, groups, [one, two], total)
    for at, out in enumerate(outs):
        out[...] = total[at]


def shards(tiles, pairs, direction):
    k_count, width, _ = tiles.shape
    cols = direction.shape[0]
    f32 = jnp.float32
    block = jax.ShapeDtypeStruct((cols, width), f32)
    smem = pl.BlockSpec(memory_space=pltpu.SMEM)
    vmem = pl.BlockSpec(memory_space=pltpu.VMEM)
    hbm = pl.BlockSpec(memory_space=pltpu.HBM)
    params = pltpu.CompilerParams(vmem_limit_bytes=VMEM_BYTES)
    x_swap = [(b, b ^ 1) for b in range(BLKS)]
    pairs = pairs.T
    lanes = pltpu.with_memory_space_constraint(direction.reshape(cols, GRPS, 4, 128), pltpu.HBM)

    own = pl.pallas_call(
        own_kernel,
        out_shape=block,
        in_specs=[hbm],
        out_specs=vmem,
        scratch_shapes=[pltpu.VMEM((cols, 4, 128), f32), pltpu.SemaphoreType.DMA],
        compiler_params=params,
        name="own",
    )(lanes)
    near_own = lax.ppermute(own, "blk", x_swap)
    got = [own, near_own]
    for step in range(1, YS):
        swap = [(b, (b + 2 * step) % BLKS) for b in range(BLKS)]
        got += [lax.ppermute(own, "blk", swap), lax.ppermute(near_own, "blk", swap)]

    rows, held = pl.pallas_call(
        rows_kernel,
        out_shape=[jax.ShapeDtypeStruct((BLKS, cols, width), f32), jax.ShapeDtypeStruct(tiles.shape, f32)],
        in_specs=[smem, hbm, hbm],
        out_specs=[vmem, vmem],
        scratch_shapes=[pltpu.VMEM((k_count, cols, 4, 128), f32), pltpu.SemaphoreType.DMA((2, k_count))],
        compiler_params=params,
        cost_estimate=pl.CostEstimate(flops=600_000_000, bytes_accessed=10_000_000, transcendentals=0),
        name="rows",
    )(pairs, lanes, pltpu.with_memory_space_constraint(tiles, pltpu.HBM))

    terms = pl.pallas_call(
        mirror_kernel,
        out_shape=jax.ShapeDtypeStruct((k_count * cols + 8, width), f32),
        in_specs=[smem] + [vmem] * (BLKS + 1),
        out_specs=vmem,
        scratch_shapes=[pltpu.VMEM((k_count, cols, width), f32)],
        compiler_params=params,
        name="mirror",
    )(pairs, *got, held)
    over_x = lax.ppermute(terms, "grp", [(g, g ^ 2) for g in range(GRPS)])
    over_core = lax.ppermute(terms, "grp", [(g, g ^ 1) for g in range(GRPS)])
    over_both = lax.ppermute(over_x, "grp", [(g, g ^ 1) for g in range(GRPS)])
    rows = lax.all_to_all(rows, "blk", 0, 0, tiled=True)
    part = pl.pallas_call(
        place_kernel,
        out_shape=jax.ShapeDtypeStruct((ZS, cols, width), f32),
        in_specs=[smem, vmem, vmem],
        out_specs=vmem,
        compiler_params=params,
        name="place",
    )(pairs, terms, over_core)
    parts = pl.pallas_call(
        join_kernel,
        out_shape=[block] * ZS,
        in_specs=[smem, vmem, vmem, vmem],
        out_specs=[vmem] * ZS,
        scratch_shapes=[pltpu.VMEM((ZS, cols, width), f32)],
        compiler_params=params,
        name="join",
    )(pairs, part, over_x, over_both)
    parts = list(parts)
    for step in Z_ORDER:
        if step in Z_AFTER:
            parts[step], parts[Z_AFTER[step]] = lax.optimization_barrier((parts[step], parts[Z_AFTER[step]]))
        parts[step] = lax.ppermute(parts[step], "grp", [(g, (g + 4 * step) % GRPS) for g in range(GRPS)])
    total = jnp.sum(rows, axis=0)
    for part in parts:
        total = total + part
    return total.reshape(cols, 1, 1, width)


def solution(mesh):
    placed = (P(("grp", "blk"), None, None), P(("grp", "blk"), None), P(None, None, "blk", None))
    return jax.shard_map(
        shards, mesh=mesh, in_specs=placed, out_specs=P(None, "grp", "blk", None), check_vma=False
    )
```

```python
import jax
import jax.numpy as jnp
from jax import lax
from jax.experimental import pallas as pl
from jax.experimental.pallas import tpu as pltpu
from jax.sharding import PartitionSpec as P

BLKS = 8
GRPS = 32
ZS = 8
YS = 4
Z_ORDER = (4, 3, 5, 2, 6, 1, 7)
Z_AFTER = {1: 2, 7: 6}
X_AFTER = 6
VMEM_BYTES = 32 * 1024 * 1024


def split(x):
    high = x.astype(jnp.bfloat16)
    low = (x - high.astype(jnp.float32)).astype(jnp.bfloat16)
    return high, low


def product(p, tile, contract):
    count = p.shape[0]
    p_parts = jnp.concatenate(split(p), axis=0)
    t_high, t_low = split(tile)
    dims = (((1,), (contract,)), ((), ()))
    first = lax.dot_general(p_parts, t_high, dims, preferred_element_type=jnp.float32)
    second = lax.dot_general(p_parts, t_low, dims, preferred_element_type=jnp.float32)
    both = first + second
    return both[:count] + both[count:]


def joined(ref):
    return jnp.concatenate([ref[:, q, :] for q in range(4)], axis=1)


def own_kernel(direction, out, own, sem):
    copy = pltpu.make_async_copy(direction.at[:, lax.axis_index("grp")], own, sem)
    copy.start()
    copy.wait()
    out[...] = joined(own)


def rows_kernel(pairs, direction, tiles, out, held, picked, sem):
    k_count = tiles.shape[0]
    picks, loads = [], []
    for k in range(k_count):
        group = pairs[1, k] // BLKS
        picks.append(pltpu.make_async_copy(direction.at[:, group], picked.at[k], sem.at[0, k]))
        loads.append(pltpu.make_async_copy(tiles.at[k], held.at[k], sem.at[1, k]))
        picks[k].start()
        loads[k].start()
    out[...] = jnp.zeros_like(out)
    for k in range(k_count):
        picks[k].wait()
        loads[k].wait()
        r, b = pairs[0, k] % BLKS, pairs[1, k] % BLKS
        out[r // 2, (r + b) % 2] += product(joined(picked.at[k]), held[k], 1)


def mirror_kernel(pairs, *refs):
    *got, tiles, out, held = refs
    k_count = tiles.shape[0]
    cols = got[0].shape[0]
    b = pairs[1, 0] % BLKS
    for k in range(k_count):
        i, j = pairs[0, k], pairs[1, k]
        r = i % BLKS
        source = (b // 2 + YS - r // 2) % YS * 2 + (r + b) % 2
        for at, block in enumerate(got):

            @pl.when(source == at)
            def _():
                held[k] = block[...]

        out[pl.ds(k * cols, cols)] = product(held[k], tiles[k], 0)
        place = jnp.where(i != j, j // BLKS, -1).astype(jnp.float32)
        out[k_count * cols:, pl.ds(k * 128, 128)] = jnp.full((8, 128), place, jnp.float32)


def group_of(part, k, k_count, cols):
    return part[pl.ds(k_count * cols, 1), pl.ds(k * 128, 128)][0, 0].astype(jnp.int32)


def add_parts(grp, groups, parts, out):
    cols = out.shape[1]
    k_count = len(groups) // len(parts)
    for at, m in enumerate(groups):

        @pl.when((m >= 0) & (m % 4 == grp % 4))
        def _():
            out[(m // 4 + ZS - grp // 4) % ZS] += parts[at // k_count][pl.ds(at % k_count * cols, cols)]


def place_kernel(pairs, own, other, out):
    cols, width = out.shape[1:]
    k_count = width // 128
    groups = [jnp.where(pairs[0, k] != pairs[1, k], pairs[1, k] // BLKS, -1) for k in range(k_count)]
    groups += [group_of(other, k, k_count, cols) for k in range(k_count)]
    out[...] = jnp.zeros_like(out)
    add_parts(pairs[0, 0] // BLKS, groups, [own, other], out)


def join_kernel(pairs, base, one, two, *refs):
    *outs, total = refs
    cols, width = total.shape[1:]
    k_count = width // 128
    groups = [group_of(part, k, k_count, cols) for part in (one, two) for k in range(k_count)]
    total[...] = base[...]
    add_parts(pairs[0, 0] // BLKS, groups, [one, two], total)
    for at, out in enumerate(outs):
        out[...] = total[at]


def shards(tiles, pairs, direction):
    k_count, width, _ = tiles.shape
    cols = direction.shape[0]
    f32 = jnp.float32
    block = jax.ShapeDtypeStruct((cols, width), f32)
    smem = pl.BlockSpec(memory_space=pltpu.SMEM)
    vmem = pl.BlockSpec(memory_space=pltpu.VMEM)
    hbm = pl.BlockSpec(memory_space=pltpu.HBM)
    params = pltpu.CompilerParams(vmem_limit_bytes=VMEM_BYTES)
    x_swap = [(b, b ^ 1) for b in range(BLKS)]
    pairs = pairs.T
    lanes = pltpu.with_memory_space_constraint(direction.reshape(cols, GRPS, 4, 128), pltpu.HBM)

    own = pl.pallas_call(
        own_kernel,
        out_shape=block,
        in_specs=[hbm],
        out_specs=vmem,
        scratch_shapes=[pltpu.VMEM((cols, 4, 128), f32), pltpu.SemaphoreType.DMA],
        compiler_params=params,
        name="own",
    )(lanes)
    near_own = lax.ppermute(own, "blk", x_swap)
    got = [own, near_own]
    for step in range(1, YS):
        swap = [(b, (b + 2 * step) % BLKS) for b in range(BLKS)]
        got += [lax.ppermute(own, "blk", swap), lax.ppermute(near_own, "blk", swap)]

    rows, held = pl.pallas_call(
        rows_kernel,
        out_shape=[jax.ShapeDtypeStruct((YS, 2, cols, width), f32), jax.ShapeDtypeStruct(tiles.shape, f32)],
        in_specs=[smem, hbm, hbm],
        out_specs=[vmem, vmem],
        scratch_shapes=[pltpu.VMEM((k_count, cols, 4, 128), f32), pltpu.SemaphoreType.DMA((2, k_count))],
        compiler_params=params,
        cost_estimate=pl.CostEstimate(flops=600_000_000, bytes_accessed=10_000_000, transcendentals=0),
        name="rows",
    )(pairs, lanes, pltpu.with_memory_space_constraint(tiles, pltpu.HBM))

    terms = pl.pallas_call(
        mirror_kernel,
        out_shape=jax.ShapeDtypeStruct((k_count * cols + 8, width), f32),
        in_specs=[smem] + [vmem] * (BLKS + 1),
        out_specs=vmem,
        scratch_shapes=[pltpu.VMEM((k_count, cols, width), f32)],
        compiler_params=params,
        name="mirror",
    )(pairs, *got, held)
    over_x = lax.ppermute(terms, "grp", [(g, g ^ 2) for g in range(GRPS)])
    over_core = lax.ppermute(terms, "grp", [(g, g ^ 1) for g in range(GRPS)])
    over_both = lax.ppermute(over_x, "grp", [(g, g ^ 1) for g in range(GRPS)])
    along_y = [[2 * y + x for y in range(YS)] for x in range(2)]
    rows = lax.all_to_all(rows, "blk", 0, 0, tiled=True, axis_index_groups=along_y)
    part = pl.pallas_call(
        place_kernel,
        out_shape=jax.ShapeDtypeStruct((ZS, cols, width), f32),
        in_specs=[smem, vmem, vmem],
        out_specs=vmem,
        compiler_params=params,
        name="place",
    )(pairs, terms, over_core)
    parts = pl.pallas_call(
        join_kernel,
        out_shape=[block] * ZS,
        in_specs=[smem, vmem, vmem, vmem],
        out_specs=[vmem] * ZS,
        scratch_shapes=[pltpu.VMEM((ZS, cols, width), f32)],
        compiler_params=params,
        name="join",
    )(pairs, part, over_x, over_both)
    parts = list(parts)
    for step in Z_ORDER:
        if step in Z_AFTER:
            parts[step], parts[Z_AFTER[step]] = lax.optimization_barrier((parts[step], parts[Z_AFTER[step]]))
        parts[step] = lax.ppermute(parts[step], "grp", [(g, (g + 4 * step) % GRPS) for g in range(GRPS)])
    rows, parts[X_AFTER] = lax.optimization_barrier((rows, parts[X_AFTER]))
    row_sum = jnp.sum(rows, axis=0)
    total = row_sum[0] + lax.ppermute(row_sum[1], "blk", x_swap)
    for part in parts:
        total = total + part
    return total.reshape(cols, 1, 1, width)


def solution(mesh):
    placed = (P(("grp", "blk"), None, None), P(("grp", "blk"), None), P(None, None, "blk", None))
    return jax.shard_map(
        shards, mesh=mesh, in_specs=placed, out_specs=P(None, "grp", "blk", None), check_vma=False
    )
```

```python
import jax
import jax.numpy as jnp
from jax import lax
from jax.experimental import pallas as pl
from jax.experimental.pallas import tpu as pltpu
from jax.sharding import PartitionSpec as P

BLKS = 8
GRPS = 32
ZS = 8
YS = 4
Z_ORDER = (4, 3, 5, 2, 6, 1, 7)
Z_AFTER = {1: 2, 7: 6}
X_AFTER = 6
VMEM_BYTES = 32 * 1024 * 1024


def split(x):
    high = x.astype(jnp.bfloat16)
    low = (x - high.astype(jnp.float32)).astype(jnp.bfloat16)
    return high, low


def product(p, tile, contract):
    count = p.shape[0]
    p_parts = jnp.concatenate(split(p), axis=0)
    t_high, t_low = split(tile)
    dims = (((1,), (contract,)), ((), ()))
    first = lax.dot_general(p_parts, t_high, dims, preferred_element_type=jnp.float32)
    second = lax.dot_general(p_parts, t_low, dims, preferred_element_type=jnp.float32)
    both = first + second
    return both[:count] + both[count:]


def joined(ref):
    return jnp.concatenate([ref[:, q, :] for q in range(4)], axis=1)


def own_kernel(direction, out, own, sem):
    copy = pltpu.make_async_copy(direction.at[:, lax.axis_index("grp")], own, sem)
    copy.start()
    copy.wait()
    out[...] = joined(own)


def rows_kernel(pairs, direction, tiles, out, held, picked, sem):
    k_count = tiles.shape[0]
    picks, loads = [], []
    for k in range(k_count):
        group = pairs[1, k] // BLKS
        picks.append(pltpu.make_async_copy(direction.at[:, group], picked.at[k], sem.at[0, k]))
        loads.append(pltpu.make_async_copy(tiles.at[k], held.at[k], sem.at[1, k]))
        picks[k].start()
        loads[k].start()
    out[...] = jnp.zeros_like(out)
    for k in range(k_count):
        picks[k].wait()
        loads[k].wait()
        r, b = pairs[0, k] % BLKS, pairs[1, k] % BLKS
        out[r // 2, (r + b) % 2] += product(joined(picked.at[k]), held[k], 1)


def mirror_kernel(pairs, *refs):
    *got, tiles, out, held = refs
    k_count = tiles.shape[0]
    cols = got[0].shape[0]
    b = pairs[1, 0] % BLKS
    for k in range(k_count):
        i, j = pairs[0, k], pairs[1, k]
        r = i % BLKS
        source = (b // 2 + YS - r // 2) % YS * 2 + (r + b) % 2
        for at, block in enumerate(got):

            @pl.when(source == at)
            def _():
                held[k] = block[...]

        out[pl.ds(k * cols, cols)] = product(held[k], tiles[k], 0)
        place = jnp.where(i != j, j // BLKS, -1).astype(jnp.float32)
        out[k_count * cols:, pl.ds(k * 128, 128)] = jnp.full((8, 128), place, jnp.float32)


def group_of(part, k, k_count, cols):
    return part[pl.ds(k_count * cols, 1), pl.ds(k * 128, 128)][0, 0].astype(jnp.int32)


def add_parts(grp, groups, parts, out):
    cols = out.shape[1]
    k_count = len(groups) // len(parts)
    for at, m in enumerate(groups):

        @pl.when((m >= 0) & (m % 4 == grp % 4))
        def _():
            out[(m // 4 + ZS - grp // 4) % ZS] += parts[at // k_count][pl.ds(at % k_count * cols, cols)]


def place_kernel(pairs, own, other, out):
    cols, width = out.shape[1:]
    k_count = width // 128
    groups = [jnp.where(pairs[0, k] != pairs[1, k], pairs[1, k] // BLKS, -1) for k in range(k_count)]
    groups += [group_of(other, k, k_count, cols) for k in range(k_count)]
    out[...] = jnp.zeros_like(out)
    add_parts(pairs[0, 0] // BLKS, groups, [own, other], out)


def join_kernel(pairs, base, one, two, *refs):
    *outs, total = refs
    cols, width = total.shape[1:]
    k_count = width // 128
    groups = [group_of(part, k, k_count, cols) for part in (one, two) for k in range(k_count)]
    total[...] = base[...]
    add_parts(pairs[0, 0] // BLKS, groups, [one, two], total)
    for at, out in enumerate(outs):
        out[...] = total[at]


def total_kernel(*refs):
    *parts, out = refs
    total = parts[0][...]
    for part in parts[1:]:
        total = total + part[...]
    for q in range(4):
        out[:, q, :] = total[:, 128 * q:128 * (q + 1)]


def shards(tiles, pairs, direction):
    k_count, width, _ = tiles.shape
    cols = direction.shape[0]
    f32 = jnp.float32
    block = jax.ShapeDtypeStruct((cols, width), f32)
    smem = pl.BlockSpec(memory_space=pltpu.SMEM)
    vmem = pl.BlockSpec(memory_space=pltpu.VMEM)
    hbm = pl.BlockSpec(memory_space=pltpu.HBM)
    params = pltpu.CompilerParams(vmem_limit_bytes=VMEM_BYTES)
    x_swap = [(b, b ^ 1) for b in range(BLKS)]
    pairs = pairs.T
    lanes = pltpu.with_memory_space_constraint(direction.reshape(cols, GRPS, 4, 128), pltpu.HBM)

    own = pl.pallas_call(
        own_kernel,
        out_shape=block,
        in_specs=[hbm],
        out_specs=vmem,
        scratch_shapes=[pltpu.VMEM((cols, 4, 128), f32), pltpu.SemaphoreType.DMA],
        compiler_params=params,
        name="own",
    )(lanes)
    near_own = lax.ppermute(own, "blk", x_swap)
    got = [own, near_own]
    for step in range(1, YS):
        swap = [(b, (b + 2 * step) % BLKS) for b in range(BLKS)]
        got += [lax.ppermute(own, "blk", swap), lax.ppermute(near_own, "blk", swap)]

    rows, held = pl.pallas_call(
        rows_kernel,
        out_shape=[jax.ShapeDtypeStruct((YS, 2, cols, width), f32), jax.ShapeDtypeStruct(tiles.shape, f32)],
        in_specs=[smem, hbm, hbm],
        out_specs=[vmem, vmem],
        scratch_shapes=[pltpu.VMEM((k_count, cols, 4, 128), f32), pltpu.SemaphoreType.DMA((2, k_count))],
        compiler_params=params,
        cost_estimate=pl.CostEstimate(flops=600_000_000, bytes_accessed=10_000_000, transcendentals=0),
        name="rows",
    )(pairs, lanes, pltpu.with_memory_space_constraint(tiles, pltpu.HBM))

    terms = pl.pallas_call(
        mirror_kernel,
        out_shape=jax.ShapeDtypeStruct((k_count * cols + 8, width), f32),
        in_specs=[smem] + [vmem] * (BLKS + 1),
        out_specs=vmem,
        scratch_shapes=[pltpu.VMEM((k_count, cols, width), f32)],
        compiler_params=params,
        name="mirror",
    )(pairs, *got, held)
    over_x = lax.ppermute(terms, "grp", [(g, g ^ 2) for g in range(GRPS)])
    over_core = lax.ppermute(terms, "grp", [(g, g ^ 1) for g in range(GRPS)])
    over_both = lax.ppermute(over_x, "grp", [(g, g ^ 1) for g in range(GRPS)])
    along_y = [[2 * y + x for y in range(YS)] for x in range(2)]
    rows = lax.all_to_all(rows, "blk", 0, 0, tiled=True, axis_index_groups=along_y)
    part = pl.pallas_call(
        place_kernel,
        out_shape=jax.ShapeDtypeStruct((ZS, cols, width), f32),
        in_specs=[smem, vmem, vmem],
        out_specs=vmem,
        compiler_params=params,
        name="place",
    )(pairs, terms, over_core)
    parts = pl.pallas_call(
        join_kernel,
        out_shape=[block] * ZS,
        in_specs=[smem, vmem, vmem, vmem],
        out_specs=[vmem] * ZS,
        scratch_shapes=[pltpu.VMEM((ZS, cols, width), f32)],
        compiler_params=params,
        name="join",
    )(pairs, part, over_x, over_both)
    parts = list(parts)
    for step in Z_ORDER:
        if step in Z_AFTER:
            parts[step], parts[Z_AFTER[step]] = lax.optimization_barrier((parts[step], parts[Z_AFTER[step]]))
        parts[step] = lax.ppermute(parts[step], "grp", [(g, (g + 4 * step) % GRPS) for g in range(GRPS)])
    rows, parts[X_AFTER] = lax.optimization_barrier((rows, parts[X_AFTER]))
    row_sum = jnp.sum(rows, axis=0)
    parts += [row_sum[0], lax.ppermute(row_sum[1], "blk", x_swap)]
    total = pl.pallas_call(
        total_kernel,
        out_shape=jax.ShapeDtypeStruct((cols, 4, 128), f32),
        in_specs=[vmem] * len(parts),
        out_specs=vmem,
        compiler_params=params,
        name="total",
    )(*parts)
    return total.reshape(cols, 1, 1, width)


def solution(mesh):
    placed = (P(("grp", "blk"), None, None), P(("grp", "blk"), None), P(None, None, "blk", None))
    return jax.shard_map(
        shards, mesh=mesh, in_specs=placed, out_specs=P(None, "grp", "blk", None), check_vma=False
    )
```

```python
import jax
import jax.numpy as jnp
from jax import lax
from jax.experimental import pallas as pl
from jax.experimental.pallas import tpu as pltpu
from jax.sharding import PartitionSpec as P

BLKS = 8
GRPS = 32
ZS = 8
YS = 4
Z_ORDER = (4, 3, 5, 2, 6, 1, 7)
Z_AFTER = {1: 2, 7: 6}
X_AFTER = 2
VMEM_BYTES = 32 * 1024 * 1024


def split(x):
    high = x.astype(jnp.bfloat16)
    low = (x - high.astype(jnp.float32)).astype(jnp.bfloat16)
    return high, low


def product(p, tile, contract):
    count = p.shape[0]
    p_parts = jnp.concatenate(split(p), axis=0)
    t_high, t_low = split(tile)
    dims = (((1,), (contract,)), ((), ()))
    first = lax.dot_general(p_parts, t_high, dims, preferred_element_type=jnp.float32)
    second = lax.dot_general(p_parts, t_low, dims, preferred_element_type=jnp.float32)
    both = first + second
    return both[:count] + both[count:]


def joined(ref):
    return jnp.concatenate([ref[:, q, :] for q in range(4)], axis=1)


def own_kernel(direction, out, own, sem):
    copy = pltpu.make_async_copy(direction.at[:, lax.axis_index("grp")], own, sem)
    copy.start()
    copy.wait()
    out[...] = joined(own)


def rows_kernel(pairs, direction, tiles, out, held, picked, sem):
    k_count = tiles.shape[0]
    picks, loads = [], []
    for k in range(k_count):
        group = pairs[1, k] // BLKS
        picks.append(pltpu.make_async_copy(direction.at[:, group], picked.at[k], sem.at[0, k]))
        loads.append(pltpu.make_async_copy(tiles.at[k], held.at[k], sem.at[1, k]))
        picks[k].start()
        loads[k].start()
    out[...] = jnp.zeros_like(out)
    for k in range(k_count):
        picks[k].wait()
        loads[k].wait()
        r, b = pairs[0, k] % BLKS, pairs[1, k] % BLKS
        out[r // 2, (r + b) % 2] += product(joined(picked.at[k]), held[k], 1)


def mirror_kernel(pairs, *refs):
    *got, tiles, out, held = refs
    k_count = tiles.shape[0]
    cols = got[0].shape[0]
    b = pairs[1, 0] % BLKS
    for k in range(k_count):
        i, j = pairs[0, k], pairs[1, k]
        r = i % BLKS
        source = (b // 2 + YS - r // 2) % YS * 2 + (r + b) % 2
        for at, block in enumerate(got):

            @pl.when(source == at)
            def _():
                held[k] = block[...]

        out[pl.ds(k * cols, cols)] = product(held[k], tiles[k], 0)
        place = jnp.where(i != j, j // BLKS, -1).astype(jnp.float32)
        out[k_count * cols:, pl.ds(k * 128, 128)] = jnp.full((8, 128), place, jnp.float32)


def group_of(part, k, k_count, cols):
    return part[pl.ds(k_count * cols, 1), pl.ds(k * 128, 128)][0, 0].astype(jnp.int32)


def add_parts(grp, groups, parts, out):
    cols = out.shape[1]
    k_count = len(groups) // len(parts)
    for at, m in enumerate(groups):

        @pl.when((m >= 0) & (m % 4 == grp % 4))
        def _():
            out[(m // 4 + ZS - grp // 4) % ZS] += parts[at // k_count][pl.ds(at % k_count * cols, cols)]


def place_kernel(pairs, own, other, out):
    cols, width = out.shape[1:]
    k_count = width // 128
    groups = [jnp.where(pairs[0, k] != pairs[1, k], pairs[1, k] // BLKS, -1) for k in range(k_count)]
    groups += [group_of(other, k, k_count, cols) for k in range(k_count)]
    out[...] = jnp.zeros_like(out)
    add_parts(pairs[0, 0] // BLKS, groups, [own, other], out)


def join_kernel(pairs, base, one, two, *refs):
    *outs, total = refs
    cols, width = total.shape[1:]
    k_count = width // 128
    groups = [group_of(part, k, k_count, cols) for part in (one, two) for k in range(k_count)]
    total[...] = base[...]
    add_parts(pairs[0, 0] // BLKS, groups, [one, two], total)
    for at, out in enumerate(outs):
        out[...] = total[at]


def shards(tiles, pairs, direction):
    k_count, width, _ = tiles.shape
    cols = direction.shape[0]
    f32 = jnp.float32
    block = jax.ShapeDtypeStruct((cols, width), f32)
    smem = pl.BlockSpec(memory_space=pltpu.SMEM)
    vmem = pl.BlockSpec(memory_space=pltpu.VMEM)
    hbm = pl.BlockSpec(memory_space=pltpu.HBM)
    params = pltpu.CompilerParams(vmem_limit_bytes=VMEM_BYTES)
    x_swap = [(b, b ^ 1) for b in range(BLKS)]
    pairs = pairs.T
    lanes = pltpu.with_memory_space_constraint(direction.reshape(cols, GRPS, 4, 128), pltpu.HBM)

    own = pl.pallas_call(
        own_kernel,
        out_shape=block,
        in_specs=[hbm],
        out_specs=vmem,
        scratch_shapes=[pltpu.VMEM((cols, 4, 128), f32), pltpu.SemaphoreType.DMA],
        compiler_params=params,
        name="own",
    )(lanes)
    near_own = lax.ppermute(own, "blk", x_swap)
    got = [own, near_own]
    for step in range(1, YS):
        swap = [(b, (b + 2 * step) % BLKS) for b in range(BLKS)]
        got += [lax.ppermute(own, "blk", swap), lax.ppermute(near_own, "blk", swap)]

    rows, held = pl.pallas_call(
        rows_kernel,
        out_shape=[jax.ShapeDtypeStruct((YS, 2, cols, width), f32), jax.ShapeDtypeStruct(tiles.shape, f32)],
        in_specs=[smem, hbm, hbm],
        out_specs=[vmem, vmem],
        scratch_shapes=[pltpu.VMEM((k_count, cols, 4, 128), f32), pltpu.SemaphoreType.DMA((2, k_count))],
        compiler_params=params,
        cost_estimate=pl.CostEstimate(flops=600_000_000, bytes_accessed=10_000_000, transcendentals=0),
        name="rows",
    )(pairs, lanes, pltpu.with_memory_space_constraint(tiles, pltpu.HBM))

    terms = pl.pallas_call(
        mirror_kernel,
        out_shape=jax.ShapeDtypeStruct((k_count * cols + 8, width), f32),
        in_specs=[smem] + [vmem] * (BLKS + 1),
        out_specs=vmem,
        scratch_shapes=[pltpu.VMEM((k_count, cols, width), f32)],
        compiler_params=params,
        name="mirror",
    )(pairs, *got, held)
    over_x = lax.ppermute(terms, "grp", [(g, g ^ 2) for g in range(GRPS)])
    over_core = lax.ppermute(terms, "grp", [(g, g ^ 1) for g in range(GRPS)])
    over_both = lax.ppermute(over_x, "grp", [(g, g ^ 1) for g in range(GRPS)])
    along_y = [[2 * y + x for y in range(YS)] for x in range(2)]
    rows = lax.all_to_all(rows, "blk", 0, 0, tiled=True, axis_index_groups=along_y)
    part = pl.pallas_call(
        place_kernel,
        out_shape=jax.ShapeDtypeStruct((ZS, cols, width), f32),
        in_specs=[smem, vmem, vmem],
        out_specs=vmem,
        compiler_params=params,
        name="place",
    )(pairs, terms, over_core)
    parts = pl.pallas_call(
        join_kernel,
        out_shape=[block] * ZS,
        in_specs=[smem, vmem, vmem, vmem],
        out_specs=[vmem] * ZS,
        scratch_shapes=[pltpu.VMEM((ZS, cols, width), f32)],
        compiler_params=params,
        name="join",
    )(pairs, part, over_x, over_both)
    parts = list(parts)
    for step in Z_ORDER:
        if step in Z_AFTER:
            parts[step], parts[Z_AFTER[step]] = lax.optimization_barrier((parts[step], parts[Z_AFTER[step]]))
        parts[step] = lax.ppermute(parts[step], "grp", [(g, (g + 4 * step) % GRPS) for g in range(GRPS)])
    rows, parts[X_AFTER] = lax.optimization_barrier((rows, parts[X_AFTER]))
    row_sum = jnp.sum(rows, axis=0)
    total = row_sum[0] + lax.ppermute(row_sum[1], "blk", x_swap)
    for part in parts:
        total = total + part
    return total.reshape(cols, 1, 1, width)


def solution(mesh):
    placed = (P(("grp", "blk"), None, None), P(("grp", "blk"), None), P(None, None, "blk", None))
    return jax.shard_map(
        shards, mesh=mesh, in_specs=placed, out_specs=P(None, "grp", "blk", None), check_vma=False
    )
```
